32 devices in a mesh: layer: 4 (over y, x), feat: 8 (over z, core).
Axes of the slice: x: 2, y: 2, z: 4, core: 2. Of those that a mesh axis runs over, the one named last changes fastest.
Arguments:
- source_decoder: bfloat16 [4, 1024, 8192], P('layer', 'feat'), may hold values from -0.0625 to 0.0625
- reader_encoder: bfloat16 [4, 8192, 6144], P('layer', None, 'feat'), may hold values from -6 to 6
- source_acts: bfloat16 [2048, 4096], P('feat', 'layer'), may hold values from 0 to 2
- target_grads: bfloat16 [2048, 24576], P('feat', 'layer'), may hold values from -0.13183594 to 0.13183594
- pair_source: int32 [4, 8, 24], P('layer', 'feat'), may hold values from 0 to 3
- pair_target: int32 [4, 8, 24], P('layer', 'feat'), may hold values from 0 to 5
- pair_count: int32 [4, 8], P('layer', 'feat'), may hold values from 1 to 24, as said below
Outputs:
- edge_table: float32 [4, 8, 24, 128, 128], P('layer', 'feat')
The draws below stay inside these ranges and needn't reach their ends.
Inputs may be any that keep to these rules, and one draw needn't show every extreme that they name: `pair_count`: slots at and past the count of a reader layer and column are unused; in every draw some reader layer and column uses all 24 slots.
All inputs are finite; a program needn't handle non-finite values.
Results may differ from the reference program's by a relative error of at most 0.0003.
Values may be sent and summed in bfloat16 or wider, within the bound.
A program may use at most 192 MiB of HBM per device.

```python
import jax
import jax.numpy as jnp
from jax import lax

D = 8192
BLK = 128
TGT_DEV = 6
CAP = 24
READERS = 4
TOKENS = 2048
N_LAYER = 4
N_FEAT = 8


def draw_pair_count(key, part):
    first_key, second_key = jax.random.split(jax.random.fold_in(key, 7))
    counts = jax.random.randint(first_key, (READERS * N_FEAT,), 1, CAP + 1)
    chosen = jax.random.randint(second_key, (), 0, READERS * N_FEAT)
    counts = counts.at[chosen].set(CAP)
    return counts.reshape(READERS, N_FEAT).astype(jnp.int32)


def with_ends(values, key, low, high):
    longest = values.shape.index(max(values.shape))
    spots = []
    for shift in (0, 1):
        where = [jax.random.randint(jax.random.fold_in(key, axis), (), 0, length) for axis, length in enumerate(values.shape)]
        where[longest] = (where[longest] + shift) % values.shape[longest]
        spots.append(tuple(where))
    return values.at[spots[0]].set(low).at[spots[1]].set(high)


def shard_levels(key, extent, shards, smallest, high):
    loudness = 1.0
    for position, blocks in shards:
        heights = jax.random.uniform(jax.random.fold_in(jax.random.fold_in(key, 6), position), (blocks,), jnp.float32, smallest / len(shards), high / len(shards))
        loudness = loudness * jnp.repeat(jnp.exp(heights), extent[position] // blocks).reshape((-1,) + (1,) * (len(extent) - 1 - position))
    return loudness


def normal_values(key, extent, scale, most, pieces=(), kind=jnp.bfloat16):
    array = scale * jax.random.normal(key, extent, jnp.float32)
    if pieces:
        array = array * shard_levels(key, extent, pieces, -0.22, 0.18)
    return jnp.clip(array, -most, most).astype(kind)


def setup_inputs(seed: int = 0) -> dict:
    splits = jax.random.split(jax.random.key(seed), 8)
    source_decoder = normal_values(splits[0], (N_LAYER, N_FEAT * BLK, D), D ** -0.5, 0.0625, ((0, 4), (1, 8)))
    reader_encoder = normal_values(splits[1], (READERS, D, N_FEAT * TGT_DEV * BLK), 1.0, 6.0, ((0, 4), (2, 8)))
    source_acts = jnp.clip(2.0 * jax.random.uniform(splits[2], (TOKENS, N_LAYER * N_FEAT * BLK), jnp.float32) ** shard_levels(splits[2], (TOKENS, N_LAYER * N_FEAT * BLK), ((0, 8), (1, 4)), -0.2, 0.2), 0.0, 2.0).astype(jnp.bfloat16)
    target_grads = normal_values(splits[3], (TOKENS, READERS * N_FEAT * TGT_DEV * BLK), (1.0 / (TOKENS ** 0.5)), 0.13183594, ((0, 8), (1, 4)))
    pair_source = with_ends(jax.random.randint(splits[4], (READERS, N_FEAT, CAP), 0, N_LAYER), jax.random.fold_in(splits[4], 1), 0, N_LAYER - 1).astype(jnp.int32)
    pair_target = with_ends(jax.random.randint(splits[5], (READERS, N_FEAT, CAP), 0, TGT_DEV), jax.random.fold_in(splits[5], 1), 0, TGT_DEV - 1).astype(jnp.int32)
    pair_count = draw_pair_count(jax.random.fold_in(splits[7], 71), 0)
    return {"source_decoder": source_decoder, "reader_encoder": reader_encoder, "source_acts": source_acts, "target_grads": target_grads, "pair_source": pair_source, "pair_target": pair_target, "pair_count": pair_count}


def reference(source_decoder, reader_encoder, source_acts, target_grads, pair_source, pair_target, pair_count):
    decoder_rows = source_decoder.reshape(N_LAYER, N_FEAT, BLK, D)
    encoder_cols = reader_encoder.reshape(READERS, D, N_FEAT, TGT_DEV, BLK)
    source_cols = source_acts.reshape(TOKENS, N_LAYER, N_FEAT, BLK)
    target_cols = target_grads.reshape(TOKENS, READERS, N_FEAT, TGT_DEV, BLK)
    sources = pair_source.reshape(-1)
    targets = pair_target.reshape(-1)

    def single_edge(flat_slot):
        reader = flat_slot // (N_FEAT * CAP)
        column = (flat_slot // CAP) % N_FEAT
        slot_pos = flat_slot % CAP
        source = sources[flat_slot]
        target = targets[flat_slot]
        virtual = jnp.dot(decoder_rows[source, column], encoder_cols[reader, :, column, target], preferred_element_type=jnp.float32)
        coact = lax.dot_general(source_cols[:, source, column], target_cols[:, reader, column, target], (((0,), (0,)), ((), ())), preferred_element_type=jnp.float32)
        product = virtual * coact
        active = slot_pos < pair_count[reader, column]
        return jnp.where(active, product, jnp.zeros_like(product))

    edge_table = lax.map(single_edge, jnp.arange(READERS * N_FEAT * CAP, dtype=jnp.int32))
    return edge_table.reshape(READERS, N_FEAT, CAP, BLK, BLK)
```

```python
import functools

import jax
import jax.numpy as jnp
from jax import lax
from jax.experimental import pallas as pl
from jax.experimental.pallas import tpu as pltpu
from jax.sharding import PartitionSpec as P

MESH = pl.DeviceIdType.MESH
K_TILE = 1024


def kernel(
    layers,
    feats,
    dec_hbm,
    enc_hbm,
    act_hbm,
    grad_hbm,
    src_ref,
    tgt_ref,
    count_ref,
    out_ref,
    dec,
    enc,
    act,
    grad,
    virt,
    coact,
    edges,
    dec_send,
    dec_recv,
    ring_send,
    ring_recv,
    act_send,
    act_recv,
    grad_send,
    grad_recv,
    local_sem,
):
    me_l = lax.axis_index("layer")
    me_f = lax.axis_index("feat")
    blk, width = dec.shape[1], dec.shape[2]
    tokens = grad.shape[1]
    cols = grad.shape[2]
    targets = cols // blk
    half = width // 2
    half_f = feats // 2
    square = layers == 4

    def peer(j):
        if square:
            y, x = me_l // 2, me_l % 2
            y = 1 - y if j & 2 else y
            x = 1 - x if j & 1 else x
            return y * 2 + x
        return (me_l + j) % layers

    def origin(j):
        return peer(j) if square else (me_l + layers - j) % layers

    direct = (1, 2) if square else tuple(range(1, layers))

    barrier = pltpu.get_barrier_semaphore()
    for j in range(1, layers):
        pl.semaphore_signal(barrier, inc=1, device_id=(peer(j), me_f), device_id_type=MESH)
    for i in range(1, feats):
        pl.semaphore_signal(
            barrier, inc=1, device_id=(me_l, (me_f + i) % feats), device_id_type=MESH
        )

    dec_own = pltpu.make_async_copy(dec_hbm.at[0], dec.at[0], local_sem.at[0])
    enc_own = pltpu.make_async_copy(enc_hbm.at[0], enc, local_sem.at[1])
    my_act = pl.ds(pl.multiple_of(me_f * blk, blk), blk)
    act_own = pltpu.make_async_copy(act_hbm.at[:, my_act], act.at[0, me_f], local_sem.at[2])
    my_grad = pl.ds(pl.multiple_of(me_f * cols, cols), cols)
    grad_own = pltpu.make_async_copy(grad_hbm.at[:, my_grad], grad.at[me_f], local_sem.at[3])

    def act_a2a(i):
        to = (me_f + i) % feats
        return pltpu.make_async_remote_copy(
            src_ref=act_hbm.at[:, pl.ds(pl.multiple_of(to * blk, blk), blk)],
            dst_ref=act.at[0, me_f],
            send_sem=act_send.at[i],
            recv_sem=act_recv.at[i],
            device_id=(me_l, to),
            device_id_type=MESH,
        )

    def grad_a2a(i):
        to = (me_f + i) % feats
        return pltpu.make_async_remote_copy(
            src_ref=grad_hbm.at[:, pl.ds(pl.multiple_of(to * cols, cols), cols)],
            dst_ref=grad.at[me_f],
            send_sem=grad_send.at[i],
            recv_sem=grad_recv.at[i],
            device_id=(me_l, to),
            device_id_type=MESH,
        )

    def dec_copy(j, h, via=None):
        columns = pl.ds(h * half, half)
        hop = j if via is None else j ^ via
        src = dec_hbm.at[0, :, columns] if via is None else dec.at[via, :, columns]
        return pltpu.make_async_remote_copy(
            src_ref=src,
            dst_ref=dec.at[j, :, columns],
            send_sem=dec_send.at[j, h],
            recv_sem=dec_recv.at[j, h],
            device_id=(peer(hop), me_f),
            device_id_type=MESH,
        )

    def act_copy(j, h, via=0):
        rows = pl.ds(h * half_f, half_f)
        return pltpu.make_async_remote_copy(
            src_ref=act.at[via, rows],
            dst_ref=act.at[j, rows],
            send_sem=ring_send.at[j, h],
            recv_sem=ring_recv.at[j, h],
            device_id=(peer(j ^ via), me_f),
            device_id_type=MESH,
        )

    enc_own.start()
    dec_own.start()
    act_own.start()
    grad_own.start()
    pl.semaphore_wait(barrier, layers + feats - 2)

    act_moves = [act_a2a(i) for i in range(1, feats)]
    grad_moves = [grad_a2a(i) for i in range(1, feats)]
    dec_moves = {}
    ring_moves = {}
    for move in act_moves:
        move.start()
    for step in (0, 1):
        for j in direct:
            h = step if j == 2 else 1 - step
            dec_moves[j, h] = dec_copy(j, h)
            dec_moves[j, h].start()
    for move in grad_moves:
        move.start()

    def multiply(j, h):
        @pl.loop(0, half // K_TILE)
        def _(step):
            depth = pl.ds(pl.multiple_of(h * half + step * K_TILE, K_TILE), K_TILE)
            virt[j] += jnp.dot(dec[j, :, depth], enc[depth, :], preferred_element_type=jnp.float32)

    def correlate(f):
        @pl.loop(0, layers)
        def _(j):
            coact[j] += lax.dot_general(
                act[j, f], grad[f], (((0,), (0,)), ((), ())), preferred_element_type=jnp.float32
            )

    virt[...] = jnp.zeros_like(virt)
    coact[...] = jnp.zeros_like(coact)

    act_own.wait()
    for move in act_moves:
        move.wait_recv()
    for h in (0, 1):
        for j in direct:
            ring_moves[j, h] = act_copy(j, h)
            ring_moves[j, h].start()

    enc_own.wait()
    dec_own.wait()
    multiply(0, 0)
    multiply(0, 1)

    if square:
        for via, h in ((1, 1), (2, 0)):
            dec_moves[via, h].wait_recv()
            dec_moves[3, h] = dec_copy(3, h, via)
            dec_moves[3, h].start()
        multiply(1, 1)
        multiply(2, 0)
        for via, h in ((1, 1), (2, 0)):
            ring_moves[via, h].wait_recv()
            ring_moves[3, h] = act_copy(3, h, via)
            ring_moves[3, h].start()
        for j, h in ((1, 0), (2, 1)):
            dec_moves[j, h].wait_recv()
            multiply(j, h)
        for j, h in ((1, 0), (2, 1), (3, 0), (3, 1)):
            ring_moves[j, h].wait_recv()
    else:
        for j in direct:
            for h in (0, 1):
                dec_moves[j, h].wait_recv()
                multiply(j, h)
        for j in direct:
            for h in (0, 1):
                ring_moves[j, h].wait_recv()

    grad_own.wait()
    correlate(me_f)
    for i in range(1, feats):
        grad_moves[i - 1].wait_recv()
        correlate((me_f + feats - i) % feats)
    if square:
        for h in (0, 1):
            dec_moves[3, h].wait_recv()
            multiply(3, h)

    for j in range(layers):
        base = origin(j) * targets if j else me_l * targets
        for t in range(targets):
            block = pl.ds(t * blk, blk)
            edges[base + t] = virt[j, :, block] * coact[j, :, block]

    live = count_ref[0, 0]

    @pl.loop(0, out_ref.shape[2])
    def _(p):
        pair = src_ref[0, 0, p] * targets + tgt_ref[0, 0, p]
        edge = edges[pair]
        out_ref[0, 0, p] = jnp.where(p < live, edge, jnp.zeros_like(edge))

    for move in act_moves + grad_moves + list(dec_moves.values()) + list(ring_moves.values()):
        move.wait_send()


def solution(mesh):
    layers, feats = mesh.shape["layer"], mesh.shape["feat"]
    in_specs = (
        P("layer", "feat", None),
        P("layer", None, "feat"),
        P("feat", "layer"),
        P("feat", "layer"),
        P("layer", "feat", None),
        P("layer", "feat", None),
        P("layer", "feat"),
    )
    out_specs = P("layer", "feat", None, None, None)

    def local(dec, enc, act, grad, src, tgt, count):
        blk, width = dec.shape[1], dec.shape[2]
        cols = enc.shape[2]
        tokens = act.shape[0]
        slots = src.shape[2]
        smem = pl.BlockSpec(memory_space=pltpu.SMEM)
        hbm = pl.BlockSpec(memory_space=pl.ANY)
        dma = pltpu.SemaphoreType.DMA
        return pl.pallas_call(
            functools.partial(kernel, layers, feats),
            out_shape=jax.ShapeDtypeStruct((1, 1, slots, blk, blk), jnp.float32),
            in_specs=[hbm] * 4 + [smem] * 3,
            out_specs=pl.BlockSpec(memory_space=pltpu.VMEM),
            scratch_shapes=[
                pltpu.VMEM((layers, blk, width), dec.dtype),
                pltpu.VMEM((width, cols), enc.dtype),
                pltpu.VMEM((layers, feats, tokens, blk), act.dtype),
                pltpu.VMEM((feats, tokens, cols), grad.dtype),
                pltpu.VMEM((layers, blk, cols), jnp.float32),
                pltpu.VMEM((layers, blk, cols), jnp.float32),
                pltpu.VMEM((layers * (cols // blk), blk, blk), jnp.float32),
                dma((layers, 2)),
                dma((layers, 2)),
                dma((layers, 2)),
                dma((layers, 2)),
                dma((feats,)),
                dma((feats,)),
                dma((feats,)),
                dma((feats,)),
                dma((4,)),
            ],
            compiler_params=pltpu.CompilerParams(
                collective_id=0, has_side_effects=True, vmem_limit_bytes=62 * 1024 * 1024
            ),
            cost_estimate=pl.CostEstimate(
                flops=2 * layers * blk * cols * (width + tokens * feats),
                bytes_accessed=2 * (width * (cols + blk) + tokens * feats * (cols + blk)),
                transcendentals=0,
            ),
        )(dec, enc, act, grad, src, tgt, count)

    return jax.shard_map(local, mesh=mesh, in_specs=in_specs, out_specs=out_specs, check_vma=False)
```

```python
import functools

import jax
import jax.numpy as jnp
from jax import lax
from jax.experimental import pallas as pl
from jax.experimental.pallas import tpu as pltpu
from jax.sharding import PartitionSpec as P

MESH = pl.DeviceIdType.MESH
K_TILE = 1024


def kernel(
    layers,
    feats,
    dec_hbm,
    enc_hbm,
    act_hbm,
    grad_hbm,
    src_ref,
    tgt_ref,
    out_ref,
    dec,
    enc,
    act,
    grad,
    virt,
    coact,
    edges,
    dec_send,
    dec_recv,
    ring_send,
    ring_recv,
    act_send,
    act_recv,
    grad_send,
    grad_recv,
    local_sem,
):
    me_l = lax.axis_index("layer")
    me_f = lax.axis_index("feat")
    blk, width = dec.shape[1], dec.shape[2]
    tokens = grad.shape[1]
    cols = grad.shape[2]
    targets = cols // blk
    square = layers == 4
    parts = 2
    piece = width // parts
    half_f = feats // 2

    def peer(j):
        if square:
            y, x = me_l // 2, me_l % 2
            y = 1 - y if j & 2 else y
            x = 1 - x if j & 1 else x
            return y * 2 + x
        return (me_l + j) % layers

    def origin(j):
        return peer(j) if square else (me_l + layers - j) % layers

    direct = (1, 2) if square else tuple(range(1, layers))

    barrier = pltpu.get_barrier_semaphore()
    for j in range(1, layers):
        pl.semaphore_signal(barrier, inc=1, device_id=(peer(j), me_f), device_id_type=MESH)
    for i in range(1, feats):
        pl.semaphore_signal(
            barrier, inc=1, device_id=(me_l, (me_f + i) % feats), device_id_type=MESH
        )

    dec_own = pltpu.make_async_copy(dec_hbm.at[0], dec.at[0], local_sem.at[0])
    enc_own = pltpu.make_async_copy(enc_hbm.at[0], enc, local_sem.at[1])
    my_act = pl.ds(pl.multiple_of(me_f * blk, blk), blk)
    act_own = pltpu.make_async_copy(act_hbm.at[:, my_act], act.at[me_f, :, pl.ds(0, blk)], local_sem.at[2])
    my_grad = pl.ds(pl.multiple_of(me_f * cols, cols), cols)
    grad_own = pltpu.make_async_copy(grad_hbm.at[:, my_grad], grad.at[me_f], local_sem.at[3])

    def act_a2a(i):
        to = (me_f + i) % feats
        return pltpu.make_async_remote_copy(
            src_ref=act_hbm.at[:, pl.ds(pl.multiple_of(to * blk, blk), blk)],
            dst_ref=act.at[me_f, :, pl.ds(0, blk)],
            send_sem=act_send.at[i],
            recv_sem=act_recv.at[i],
            device_id=(me_l, to),
            device_id_type=MESH,
        )

    def grad_a2a(i):
        to = (me_f + i) % feats
        return pltpu.make_async_remote_copy(
            src_ref=grad_hbm.at[:, pl.ds(pl.multiple_of(to * cols, cols), cols)],
            dst_ref=grad.at[me_f],
            send_sem=grad_send.at[i],
            recv_sem=grad_recv.at[i],
            device_id=(me_l, to),
            device_id_type=MESH,
        )

    def dec_copy(j, h, via=None):
        columns = pl.ds(h * piece, piece)
        hop = j if via is None else j ^ via
        src = dec_hbm.at[0, :, columns] if via is None else dec.at[via, :, columns]
        return pltpu.make_async_remote_copy(
            src_ref=src,
            dst_ref=dec.at[j, :, columns],
            send_sem=dec_send.at[j, h],
            recv_sem=dec_recv.at[j, h],
            device_id=(peer(hop), me_f),
            device_id_type=MESH,
        )

    def act_copy(j, h, via=0):
        rows = pl.ds(h * half_f, half_f)
        return pltpu.make_async_remote_copy(
            src_ref=act.at[rows, :, pl.ds(via * blk, blk)],
            dst_ref=act.at[rows, :, pl.ds(j * blk, blk)],
            send_sem=ring_send.at[j, h],
            recv_sem=ring_recv.at[j, h],
            device_id=(peer(j ^ via), me_f),
            device_id_type=MESH,
        )

    enc_own.start()
    dec_own.start()
    act_own.start()
    grad_own.start()
    pl.semaphore_wait(barrier, layers + feats - 2)

    act_moves = [act_a2a(i) for i in range(1, feats)]
    grad_moves = [grad_a2a(i) for i in range(1, feats)]
    dec_moves = {}
    ring_moves = {}
    for move in act_moves:
        move.start()
    turns = {1: (1, 0), 2: (0, 1)}

    def send_own(step):
        for j in direct:
            h = turns[j][step] if square else step
            dec_moves[j, h] = dec_copy(j, h)
            dec_moves[j, h].start()

    for step in range(parts):
        send_own(step)
    for move in grad_moves:
        move.start()

    def multiply(j, h):
        @pl.loop(0, piece // K_TILE)
        def _(step):
            depth = pl.ds(pl.multiple_of(h * piece + step * K_TILE, K_TILE), K_TILE)
            virt[j] += jnp.dot(dec[j, :, depth], enc[depth, :], preferred_element_type=jnp.float32)

    def correlate(f):
        coact[...] += lax.dot_general(
            act[f], grad[f], (((0,), (0,)), ((), ())), preferred_element_type=jnp.float32
        )

    def receive(j, h):
        dec_moves[j, h].wait_recv()
        multiply(j, h)

    def receive_grad(i):
        grad_moves[i - 1].wait_recv()
        correlate((me_f + feats - i) % feats)

    arrivals = [i for k in range(1, feats // 2) for i in (k, feats - k)] + [feats // 2]

    virt[...] = jnp.zeros_like(virt)
    coact[...] = jnp.zeros_like(coact)
    act_own.wait()
    for move in act_moves:
        move.wait_recv()
    for h in (0, 1):
        for j in direct:
            part = 1 - h if j == 1 else h
            ring_moves[j, part] = act_copy(j, part)
            ring_moves[j, part].start()

    enc_own.wait()
    dec_own.wait()
    for h in range(parts):
        multiply(0, h)


    if square:
        for via, h in ((1, 1), (2, 0)):
            ring_moves[via, h].wait_recv()
            ring_moves[3, h] = act_copy(3, h, via)
            ring_moves[3, h].start()
        for step in (0,):
            ready = ((1, turns[1][step]), (2, turns[2][step]))
            for via, h in ready:
                dec_moves[via, h].wait_recv()
                dec_moves[3, h] = dec_copy(3, h, via)
                dec_moves[3, h].start()
            for key in ready:
                multiply(*key)
        for key in ((1, 0), (2, 1)):
            receive(*key)
        for key in ((1, 0), (2, 1), (3, 0), (3, 1)):
            ring_moves[key].wait_recv()
        last = ((3, 0), (3, 1))
    else:
        for j in direct:
            for h in (0, 1):
                ring_moves[j, h].wait_recv()
        last = tuple((j, h) for j in direct for h in (0, 1))

    grad_own.wait()
    correlate(me_f)
    for i in arrivals[:4]:
        receive_grad(i)
    for key in last[:2]:
        receive(*key)
    for i in arrivals[4:]:
        receive_grad(i)
    for key in last[2:]:
        receive(*key)

    for j in range(layers):
        base = origin(j) * targets if j else me_l * targets
        for t in range(targets):
            block = pl.ds(t * blk, blk)
            edges[base + t] = virt[j, :, block] * coact[pl.ds(j * blk, blk), block]

    @pl.loop(0, out_ref.shape[2])
    def _(p):
        out_ref[0, 0, p] = edges[src_ref[0, 0, p] * targets + tgt_ref[0, 0, p]]

    for move in act_moves + grad_moves + list(dec_moves.values()) + list(ring_moves.values()):
        move.wait_send()


def solution(mesh):
    layers, feats = mesh.shape["layer"], mesh.shape["feat"]
    in_specs = (
        P("layer", "feat", None),
        P("layer", None, "feat"),
        P("feat", "layer"),
        P("feat", "layer"),
        P("layer", "feat", None),
        P("layer", "feat", None),
        P("layer", "feat"),
    )
    out_specs = P("layer", "feat", None, None, None)

    def local(dec, enc, act, grad, src, tgt, count):
        blk, width = dec.shape[1], dec.shape[2]
        cols = enc.shape[2]
        tokens = act.shape[0]
        slots = src.shape[2]
        smem = pl.BlockSpec(memory_space=pltpu.SMEM)
        hbm = pl.BlockSpec(memory_space=pl.ANY)
        dma = pltpu.SemaphoreType.DMA
        edges = pl.pallas_call(
            functools.partial(kernel, layers, feats),
            out_shape=jax.ShapeDtypeStruct((1, 1, slots, blk, blk), jnp.float32),
            in_specs=[hbm] * 4 + [smem] * 2,
            out_specs=pl.BlockSpec(memory_space=pltpu.VMEM),
            scratch_shapes=[
                pltpu.VMEM((layers, blk, width), dec.dtype),
                pltpu.VMEM((width, cols), enc.dtype),
                pltpu.VMEM((feats, tokens, layers * blk), act.dtype),
                pltpu.VMEM((feats, tokens, cols), grad.dtype),
                pltpu.VMEM((layers, blk, cols), jnp.float32),
                pltpu.VMEM((layers * blk, cols), jnp.float32),
                pltpu.VMEM((layers * (cols // blk), blk, blk), jnp.float32),
                dma((layers, 4)),
                dma((layers, 4)),
                dma((layers, 2)),
                dma((layers, 2)),
                dma((feats,)),
                dma((feats,)),
                dma((feats,)),
                dma((feats,)),
                dma((4,)),
            ],
            compiler_params=pltpu.CompilerParams(
                collective_id=0, has_side_effects=True, vmem_limit_bytes=62 * 1024 * 1024
            ),
            cost_estimate=pl.CostEstimate(
                flops=2 * layers * blk * cols * (width + tokens * feats),
                bytes_accessed=2 * (width * (cols + blk) + tokens * feats * (cols + blk)),
                transcendentals=0,
            ),
        )(dec, enc, act, grad, src, tgt)
        live = jnp.arange(slots)[None, None, :, None, None] < count[:, :, None, None, None]
        return jnp.where(live, edges, 0.0)

    return jax.shard_map(local, mesh=mesh, in_specs=in_specs, out_specs=out_specs, check_vma=False)
```

```python
import functools

import jax
import jax.numpy as jnp
from jax import lax
from jax.experimental import pallas as pl
from jax.experimental.pallas import tpu as pltpu
from jax.sharding import PartitionSpec as P

MESH = pl.DeviceIdType.MESH
K_TILE = 1024


def kernel(
    layers,
    feats,
    dec_hbm,
    enc_hbm,
    act_hbm,
    grad_hbm,
    src_ref,
    tgt_ref,
    out_ref,
    dec,
    enc,
    act,
    grad,
    virt,
    coact,
    edges,
    dec_send,
    dec_recv,
    ring_send,
    ring_recv,
    act_send,
    act_recv,
    grad_send,
    grad_recv,
    local_sem,
):
    me_l = lax.axis_index("layer")
    me_f = lax.axis_index("feat")
    blk, width = dec.shape[1], dec.shape[2]
    tokens = grad.shape[1]
    cols = grad.shape[2]
    targets = cols // blk
    square = layers == 4
    parts = 2
    piece = width // parts
    half_f = feats // 2

    def peer(j):
        if square:
            y, x = me_l // 2, me_l % 2
            y = 1 - y if j & 2 else y
            x = 1 - x if j & 1 else x
            return y * 2 + x
        return (me_l + j) % layers

    def origin(j):
        return peer(j) if square else (me_l + layers - j) % layers

    direct = (1, 2) if square else tuple(range(1, layers))

    barrier = pltpu.get_barrier_semaphore()
    for j in range(1, layers):
        pl.semaphore_signal(barrier, inc=1, device_id=(peer(j), me_f), device_id_type=MESH)
    for i in range(1, feats):
        pl.semaphore_signal(
            barrier, inc=1, device_id=(me_l, (me_f + i) % feats), device_id_type=MESH
        )

    dec_own = pltpu.make_async_copy(dec_hbm.at[0], dec.at[0], local_sem.at[0])
    enc_own = pltpu.make_async_copy(enc_hbm.at[0], enc, local_sem.at[1])
    my_act = pl.ds(pl.multiple_of(me_f * blk, blk), blk)
    act_own = pltpu.make_async_copy(act_hbm.at[:, my_act], act.at[me_f, :, pl.ds(0, blk)], local_sem.at[2])
    my_grad = pl.ds(pl.multiple_of(me_f * cols, cols), cols)
    grad_own = pltpu.make_async_copy(grad_hbm.at[:, my_grad], grad.at[me_f], local_sem.at[3])

    def act_a2a(i):
        to = (me_f + i) % feats
        return pltpu.make_async_remote_copy(
            src_ref=act_hbm.at[:, pl.ds(pl.multiple_of(to * blk, blk), blk)],
            dst_ref=act.at[me_f, :, pl.ds(0, blk)],
            send_sem=act_send.at[i],
            recv_sem=act_recv.at[i],
            device_id=(me_l, to),
            device_id_type=MESH,
        )

    def grad_a2a(i):
        to = (me_f + i) % feats
        return pltpu.make_async_remote_copy(
            src_ref=grad_hbm.at[:, pl.ds(pl.multiple_of(to * cols, cols), cols)],
            dst_ref=grad.at[me_f],
            send_sem=grad_send.at[i],
            recv_sem=grad_recv.at[i],
            device_id=(me_l, to),
            device_id_type=MESH,
        )

    def dec_copy(j, h, via=None):
        columns = pl.ds(h * piece, piece)
        hop = j if via is None else j ^ via
        src = dec_hbm.at[0, :, columns] if via is None else dec.at[via, :, columns]
        return pltpu.make_async_remote_copy(
            src_ref=src,
            dst_ref=dec.at[j, :, columns],
            send_sem=dec_send.at[j, h],
            recv_sem=dec_recv.at[j, h],
            device_id=(peer(hop), me_f),
            device_id_type=MESH,
        )

    def act_copy(j, h, via=0):
        rows = pl.ds(h * half_f, half_f)
        return pltpu.make_async_remote_copy(
            src_ref=act.at[rows, :, pl.ds(via * blk, blk)],
            dst_ref=act.at[rows, :, pl.ds(j * blk, blk)],
            send_sem=ring_send.at[j, h],
            recv_sem=ring_recv.at[j, h],
            device_id=(peer(j ^ via), me_f),
            device_id_type=MESH,
        )

    enc_own.start()
    dec_own.start()
    act_own.start()
    grad_own.start()
    pl.semaphore_wait(barrier, layers + feats - 2)

    act_moves = [act_a2a(i) for i in range(1, feats)]
    grad_moves = [grad_a2a(i) for i in range(1, feats)]
    dec_moves = {}
    ring_moves = {}
    for move in act_moves:
        move.start()
    turns = {1: (1, 0), 2: (0, 1)}

    def send_own(step):
        for j in direct:
            h = turns[j][step] if square else step
            dec_moves[j, h] = dec_copy(j, h)
            dec_moves[j, h].start()

    for step in range(parts):
        send_own(step)
    for move in grad_moves:
        move.start()

    def multiply(j, h):
        @pl.loop(0, piece // K_TILE)
        def _(step):
            depth = pl.ds(pl.multiple_of(h * piece + step * K_TILE, K_TILE), K_TILE)
            virt[j] += jnp.dot(dec[j, :, depth], enc[depth, :], preferred_element_type=jnp.float32)

    def correlate(f):
        coact[...] += lax.dot_general(
            act[f], grad[f], (((0,), (0,)), ((), ())), preferred_element_type=jnp.float32
        )

    def receive(j, h):
        dec_moves[j, h].wait_recv()
        multiply(j, h)

    def receive_grad(i):
        grad_moves[i - 1].wait_recv()
        correlate((me_f + feats - i) % feats)

    arrivals = [i for k in range(1, feats // 2) for i in (k, feats - k)] + [feats // 2]

    virt[...] = jnp.zeros_like(virt)
    coact[...] = jnp.zeros_like(coact)
    act_own.wait()
    for move in act_moves:
        move.wait_recv()
    for h in (0, 1):
        for j in direct:
            part = 1 - h if j == 1 else h
            ring_moves[j, part] = act_copy(j, part)
            ring_moves[j, part].start()

    enc_own.wait()
    dec_own.wait()
    for h in range(parts):
        multiply(0, h)


    if square:
        for via, h in ((1, 1), (2, 0)):
            ring_moves[via, h].wait_recv()
            ring_moves[3, h] = act_copy(3, h, via)
            ring_moves[3, h].start()
        for step in (0,):
            ready = ((1, turns[1][step]), (2, turns[2][step]))
            for via, h in ready:
                dec_moves[via, h].wait_recv()
                dec_moves[3, h] = dec_copy(3, h, via)
                dec_moves[3, h].start()
            for key in ready:
                multiply(*key)
        for key in ((1, 0), (2, 1)):
            receive(*key)
        for key in ((1, 0), (2, 1), (3, 0), (3, 1)):
            ring_moves[key].wait_recv()
        last = ((3, 0), (3, 1))
    else:
        for j in direct:
            for h in (0, 1):
                ring_moves[j, h].wait_recv()
        last = tuple((j, h) for j in direct for h in (0, 1))

    grad_own.wait()
    correlate(me_f)
    for i in arrivals:
        receive_grad(i)
    for key in last:
        receive(*key)

    for j in range(layers):
        base = origin(j) * targets if j else me_l * targets
        for t in range(targets):
            block = pl.ds(t * blk, blk)
            edges[base + t] = virt[j, :, block] * coact[pl.ds(j * blk, blk), block]

    @pl.loop(0, out_ref.shape[2])
    def _(p):
        out_ref[0, 0, p] = edges[src_ref[0, 0, p] * targets + tgt_ref[0, 0, p]]

    for move in act_moves + grad_moves + list(dec_moves.values()) + list(ring_moves.values()):
        move.wait_send()


def solution(mesh):
    layers, feats = mesh.shape["layer"], mesh.shape["feat"]
    in_specs = (
        P("layer", "feat", None),
        P("layer", None, "feat"),
        P("feat", "layer"),
        P("feat", "layer"),
        P("layer", "feat", None),
        P("layer", "feat", None),
        P("layer", "feat"),
    )
    out_specs = P("layer", "feat", None, None, None)

    def local(dec, enc, act, grad, src, tgt, count):
        blk, width = dec.shape[1], dec.shape[2]
        cols = enc.shape[2]
        tokens = act.shape[0]
        slots = src.shape[2]
        smem = pl.BlockSpec(memory_space=pltpu.SMEM)
        hbm = pl.BlockSpec(memory_space=pl.ANY)
        dma = pltpu.SemaphoreType.DMA
        edges = pl.pallas_call(
            functools.partial(kernel, layers, feats),
            out_shape=jax.ShapeDtypeStruct((1, 1, slots, blk, blk), jnp.float32),
            in_specs=[hbm] * 4 + [smem] * 2,
            out_specs=pl.BlockSpec(memory_space=pltpu.VMEM),
            scratch_shapes=[
                pltpu.VMEM((layers, blk, width), dec.dtype),
                pltpu.VMEM((width, cols), enc.dtype),
                pltpu.VMEM((feats, tokens, layers * blk), act.dtype),
                pltpu.VMEM((feats, tokens, cols), grad.dtype),
                pltpu.VMEM((layers, blk, cols), jnp.float32),
                pltpu.VMEM((layers * blk, cols), jnp.float32),
                pltpu.VMEM((layers * (cols // blk), blk, blk), jnp.float32),
                dma((layers, 4)),
                dma((layers, 4)),
                dma((layers, 2)),
                dma((layers, 2)),
                dma((feats,)),
                dma((feats,)),
                dma((feats,)),
                dma((feats,)),
                dma((4,)),
            ],
            compiler_params=pltpu.CompilerParams(
                collective_id=0, has_side_effects=True, vmem_limit_bytes=62 * 1024 * 1024
            ),
            cost_estimate=pl.CostEstimate(
                flops=2 * layers * blk * cols * (width + tokens * feats),
                bytes_accessed=2 * (width * (cols + blk) + tokens * feats * (cols + blk)),
                transcendentals=0,
            ),
        )(dec, enc, act, grad, src, tgt)
        live = jnp.arange(slots)[None, None, :, None, None] < count[:, :, None, None, None]
        return jnp.where(live, edges, 0.0)

    return jax.shard_map(local, mesh=mesh, in_specs=in_specs, out_specs=out_specs, check_vma=False)
```
